32 devices in a mesh: grp: 2 (over y), mesh: 4 (over z), chaos: 2 (over x), kl: 2 (over core).
Axes of the slice: x: 2, y: 2, z: 4, core: 2. Of those that a mesh axis runs over, the one named last changes fastest.
Arguments:
- right_side: float32 [44, 2048], P(('grp', 'chaos'), 'mesh'), parts along dimension 0, may hold values from -14 to 14
- preconditioner: float32 [22, 2048], P('chaos', 'mesh'), may hold values from 0.15 to 0.6
- mass_diag: float32 [2048], P('mesh'), may hold values from 0.5 to 2
- halo_lists: int32 [2, 256], P(None, 'mesh'), may hold values from 0 to 511, as said below
- connectivity: int32 [4, 10240], P(None, 'mesh'), may hold values from 0 to 639
- gradients: float32 [3, 4, 10240], P(None, None, 'mesh'), may hold values from -0.9 to 0.9
- coefficient: float32 [20, 10240], P(('grp', 'kl'), 'mesh'), parts along dimension 0, may hold values from -0.2 to 4, as said below
- term_index: int32 [9, 2, 22], replicated, may hold values from 0 to 21, each once within a row
- term_value: float32 [9, 2, 22], replicated, may hold values from -1 to 1
Outputs:
- solution: float32 [44, 2048], P(('grp', 'chaos'), 'mesh'), parts along dimension 0
- residual: float32 [44, 2048], P(('grp', 'chaos'), 'mesh'), parts along dimension 0
The draws below stay inside these ranges and needn't reach their ends.
There are 2 independent parts, one for each index of `grp`. The reference program is written for one: setup_inputs(seed, part) draws one part's arguments, and reference() takes and returns one part's arrays. A program takes and returns all parts, laid end to end along the dimension named above; an argument that names none is the same for every part. Nothing has to cross between parts.
Inputs may be any that keep to these rules, and one draw needn't show every extreme that they name: `halo_lists`: for every partition the 64 nodes of row 0 and the 64 nodes of row 1 are 128 different local nodes. `term_index`: for each random term and slot, the column modes over all row modes are a permutation of the modes. `coefficient`: row 0 lies in 1 to 4; each other row's entry is at most 0.05 times row 0's in magnitude.
All inputs are finite; a program needn't handle non-finite values.
Results may differ from the reference program's by a relative error of at most 0.0003.
Values sent between devices are 32-bit elements; how exact they have to be, the bound alone decides.
A program may use at most 128 MiB of HBM per device.

```python
import math
import jax
import jax.numpy as jnp
from jax import lax

MODES = 22
KL = 10
NNZ = 2
NODE_DEV = 512
HALO = 64
EXT = 640
ELEM_DEV = 2560
NODES = 2048
ELEMS = 10240
ITERS = 3
N_MESH = 4


def draw_right_side(key, part):
    key = jax.random.fold_in(key, 11)
    node_pos = lax.broadcasted_iota(jnp.float32, (MODES, NODES), 1) / NODES
    mode_pos = lax.broadcasted_iota(jnp.float32, (MODES, NODES), 0) / MODES
    scale = jnp.exp(node_pos * math.log(3.0) + mode_pos * math.log(1.5))
    base = jnp.clip(jax.random.normal(key, (MODES, NODES), jnp.float32), -3.0, 3.0)
    return base * scale


def draw_halo_lists(key, part):
    key = jax.random.fold_in(key, 12)
    keys = jax.random.split(key, N_MESH)
    chosen = jax.vmap(lambda single: jax.random.permutation(single, NODE_DEV)[:2 * HALO])(keys)
    chosen = chosen.astype(jnp.int32).reshape(N_MESH, 2, HALO)
    return jnp.transpose(chosen, (1, 0, 2)).reshape(2, N_MESH * HALO)


def draw_coefficient(key, part):
    key = jax.random.fold_in(key, 13)
    mean_part = jnp.exp(jax.random.uniform(jax.random.fold_in(key, 1), (1, ELEMS), jnp.float32, 0.0, math.log(4.0)))
    ratio = jax.random.uniform(jax.random.fold_in(key, 4), (KL - 1, ELEMS), jnp.float32, -1.0, 1.0)
    return jnp.concatenate([mean_part, 0.05 * mean_part * ratio], axis=0)


def plant(drawn, stream_key, smallest, largest):
    extent = drawn.shape
    index_at = [jax.random.randint(jax.random.fold_in(stream_key, axis), (), 0, extent[axis]) for axis in range(len(extent))]
    drawn = drawn.at[tuple(index_at)].set(smallest)
    longest = extent.index(max(extent))
    index_at[longest] = (index_at[longest] + 1) % extent[longest]
    return drawn.at[tuple(index_at)].set(largest)


def steps_of(rng, dims, pieces, low, top_value):
    gain = 1.0
    for axis_at, shards_of in pieces:
        steps = jax.random.uniform(jax.random.fold_in(jax.random.fold_in(rng, 6), axis_at), (shards_of,), jnp.float32, low / len(pieces), top_value / len(pieces))
        gain = gain * jnp.repeat(jnp.exp(steps), dims[axis_at] // shards_of).reshape((-1,) + (1,) * (len(dims) - 1 - axis_at))
    return gain


def gaussian(rng, extent, deviation, limit, pieces=(), kind=jnp.bfloat16):
    factor_of = steps_of(rng, extent, pieces, -0.22, 0.18) if pieces else 1.0
    array = jax.random.normal(rng, extent, jnp.float32) * deviation * factor_of
    return jnp.minimum(jnp.maximum(array, -limit), limit).astype(kind)


def setup_inputs(seed: int = 0, part: int = 0) -> dict:
    seeds = jax.random.split(jax.random.key(seed), 10)
    part_splits = jax.random.split(jax.random.fold_in(seeds[9], part), 10)
    return {
        "right_side": draw_right_side(jax.random.fold_in(jax.random.fold_in(seeds[9], part), 71), part),
        "preconditioner": jnp.clip(jnp.exp(math.log(0.6) - 1.3862944 * jax.random.uniform(seeds[1], (MODES, NODES), jnp.float32) ** steps_of(seeds[1], (MODES, NODES), ((0, 2), (1, 4)), -0.2, 0.2)), 0.15, 0.6),
        "mass_diag": jnp.clip(jnp.exp(math.log(2.0) - 1.3862944 * jax.random.uniform(seeds[2], (NODES,), jnp.float32) ** steps_of(seeds[2], (NODES,), ((0, 4),), -0.2, 0.2)), 0.5, 2.0),
        "halo_lists": draw_halo_lists(jax.random.fold_in(seeds[9], 71), part),
        "connectivity": plant(jax.random.randint(seeds[4], (4, ELEMS), 0, EXT), jax.random.fold_in(seeds[4], 1), 0, EXT - 1).astype(jnp.int32),
        "gradients": gaussian(seeds[5], (3, 4, ELEMS), 0.15, 0.9, ((2, 4),), jnp.float32),
        "coefficient": draw_coefficient(jax.random.fold_in(jax.random.fold_in(seeds[9], part), 71), part),
        "term_index": jax.vmap(lambda own: jax.random.permutation(own, MODES))(jax.random.split(seeds[7], (KL - 1) * NNZ)).reshape((KL - 1, NNZ, MODES)).astype(jnp.int32),
        "term_value": jnp.clip(jax.random.uniform(seeds[8], (KL - 1, NNZ, MODES), jnp.float32, -1.0, 1.0), -1.0, 1.0),
    }


highest = lax.Precision.HIGHEST


def couple_terms(term_index, term_value):
    mode_count = term_index.shape[-1]
    columns = lax.broadcasted_iota(jnp.int32, term_index.shape + (mode_count,), 3)
    dense_table = jnp.sum(jnp.where(term_index[..., None] == columns, term_value[..., None], jnp.zeros((), term_value.dtype)), axis=1)
    mirror = 0.5 * (dense_table + jnp.swapaxes(dense_table, 1, 2))
    return jnp.concatenate([jnp.eye(mode_count, dtype=term_value.dtype)[None], mirror], axis=0)


def element_apply(extended, connect, gradients):
    picked = extended[:, connect]
    projected = jnp.einsum('dbe,rbe->rde', gradients, picked, precision=highest)
    return jnp.einsum('dae,rde->rae', gradients, projected, precision=highest)


def assemble(values, connect, weight, ext_width):
    row_count = values.shape[0]
    scaled = (values * weight[None, None, :]).reshape(row_count, -1)
    return jnp.zeros((row_count, ext_width), values.dtype).at[:, connect.reshape(-1)].add(scaled)


def operate(vector, mass_diag, halo_lists, connectivity, gradients, coefficient, coupling):
    mode_count = vector.shape[0]
    blocks = vector.reshape(mode_count, N_MESH, NODE_DEV)
    down_list = halo_lists[0].reshape(N_MESH, HALO)
    up_list = halo_lists[1].reshape(N_MESH, HALO)
    partition = jnp.arange(N_MESH, dtype=jnp.int32)[:, None]
    send_down = blocks[:, partition, down_list]
    send_up = blocks[:, partition, up_list]
    zero_rim = jnp.zeros((mode_count, 1, HALO), vector.dtype)
    from_lower = jnp.concatenate([zero_rim, send_up[:, :-1]], axis=1)
    from_upper = jnp.concatenate([send_down[:, 1:], zero_rim], axis=1)
    extended = jnp.concatenate([blocks, from_lower, from_upper], axis=2).transpose(1, 0, 2)
    connect = connectivity.reshape(4, N_MESH, ELEM_DEV).transpose(1, 0, 2)
    grads_part = gradients.reshape(3, 4, N_MESH, ELEM_DEV).transpose(2, 0, 1, 3)
    coef_part = coefficient.reshape(KL, N_MESH, ELEM_DEV).transpose(1, 0, 2)

    def one_partition(packed):
        ext_part, conn_part, grad_part, weight_part = packed
        element_values = element_apply(ext_part, conn_part, grad_part)
        running = jnp.zeros((mode_count, EXT), vector.dtype)
        for term_id in range(KL):
            running = running + jnp.dot(coupling[term_id], assemble(element_values, conn_part, weight_part[term_id], EXT), precision=highest)
        return running

    summed = lax.map(one_partition, (extended, connect, grads_part, coef_part))
    owned = summed[:, :, :NODE_DEV]
    back_lower = summed[:, :, NODE_DEV:NODE_DEV + HALO]
    back_upper = summed[:, :, NODE_DEV + HALO:]
    zero_back = jnp.zeros((1, mode_count, HALO), vector.dtype)
    into_up = jnp.concatenate([back_lower[1:], zero_back], axis=0)
    into_down = jnp.concatenate([zero_back, back_upper[:-1]], axis=0)

    def add_back(own_rows, up_rows, down_rows, up_vals, down_vals):
        return own_rows.at[:, up_rows].add(up_vals).at[:, down_rows].add(down_vals)

    owned = jax.vmap(add_back)(owned, up_list, down_list, into_up, into_down)
    return owned.transpose(1, 0, 2).reshape(mode_count, N_MESH * NODE_DEV) + mass_diag[None, :] * vector


def reference(right_side, preconditioner, mass_diag, halo_lists, connectivity, gradients, coefficient, term_index, term_value):
    coupling = couple_terms(term_index, term_value)

    def operator(vector):
        return operate(vector, mass_diag, halo_lists, connectivity, gradients, coefficient, coupling)

    solution = jnp.zeros_like(right_side)
    residual = right_side
    precond_res = preconditioner * residual
    image = operator(precond_res)
    dir_image = jnp.zeros_like(right_side)
    dir_precond = jnp.zeros_like(right_side)
    dir_residual = jnp.zeros_like(right_side)
    direction = jnp.zeros_like(right_side)
    gamma_old = None
    alpha_old = None
    for step_id in range(ITERS):
        gamma_now = jnp.sum(residual * precond_res)
        delta_now = jnp.sum(image * precond_res)
        scaled_image = preconditioner * image
        product = operator(scaled_image)
        if step_id == 0:
            beta_now = jnp.zeros((), right_side.dtype)
            alpha_now = gamma_now / delta_now
        else:
            beta_now = gamma_now / gamma_old
            alpha_now = gamma_now / (delta_now - beta_now * gamma_now / alpha_old)
        dir_image = product + beta_now * dir_image
        dir_precond = scaled_image + beta_now * dir_precond
        dir_residual = image + beta_now * dir_residual
        direction = precond_res + beta_now * direction
        solution = solution + alpha_now * direction
        residual = residual - alpha_now * dir_residual
        precond_res = precond_res - alpha_now * dir_precond
        image = image - alpha_now * dir_image
        gamma_old = gamma_now
        alpha_old = alpha_now
    return solution, residual
```

```python
import functools

import jax
import jax.numpy as jnp
from jax import lax
from jax.experimental import pallas as pl
from jax.experimental.pallas import tpu as pltpu
from jax.sharding import PartitionSpec as P

ITERS = 3
OPS = ITERS
F32 = jnp.float32
BF16 = jnp.bfloat16
MESH = pl.DeviceIdType.MESH


def round_up(value, unit):
    return -(-value // unit) * unit


def split(value, parts):
    pieces = []
    rest = value
    for _ in range(parts - 1):
        high = rest.astype(BF16).astype(F32)
        pieces.append(high)
        rest = rest - high
    pieces.append(rest)
    return jnp.concatenate(pieces, axis=0).astype(BF16)


def fold(value, rows):
    total = value[:rows]
    for start in range(rows, value.shape[0], rows):
        total = total + value[start : start + rows]
    return total


def dot(left, right):
    return lax.dot_general(left, right, (((1,), (0,)), ((), ())), preferred_element_type=F32)


def dot_t(left, right):
    return lax.dot_general(left, right, (((1,), (1,)), ((), ())), preferred_element_type=F32)


def kernel(
    dims,
    rhs_in,
    pre_in,
    mass_in,
    halo_in,
    conn_in,
    grad_in,
    coef_in,
    mix_in,
    x_out,
    res_out,
    gathered,
    coefs,
    dstack,
    dsend,
    zinit,
    ids,
    oht,
    halo_oh,
    base,
    mass_ext,
    mix,
    sc_hi,
    sc_lo,
    loc,
    part,
    from_x,
    from_z,
    dot_send,
    dot_recv,
    sem_gs,
    sem_gr,
    sem_cs,
    sem_cr,
    sem_zis,
    sem_zir,
    sem_xs,
    sem_xr,
    sem_zs,
    sem_zr,
    sem_ds,
    sem_dr,
):
    n_mesh, n_chaos, n_kl, modes, mode_dev, node, halo, elems, chunk, terms, term_dev = dims
    rows = round_up(modes, 8)
    rd = round_up(mode_dev, 8)
    pairs = round_up(terms, 2)
    wide = node + 4 * halo
    low_at, up_at = node, node + 2 * halo

    m = lax.axis_index("mesh")
    c = lax.axis_index("chaos")
    k = lax.axis_index("kl")
    has_low = m > 0
    has_up = m < n_mesh - 1
    sides = ((0, has_low, m - 1), (1, has_up, m + 1))

    def peer_c(off):
        return lax.rem(c + off, n_chaos)

    def source_c(off):
        return lax.rem(c + n_chaos - off, n_chaos)

    barrier = pltpu.get_barrier_semaphore()

    def greet(target):
        pl.semaphore_signal(barrier, inc=1, device_id=target, device_id_type=MESH)

    for off in range(1, n_chaos):
        greet({"chaos": peer_c(off)})
    for off in range(1, n_mesh):
        greet({"mesh": lax.rem(m + off, n_mesh)})
    for off in range(1, n_kl):
        greet({"kl": lax.rem(k + off, n_kl)})
    for _, has, other in sides:
        @pl.when(has)
        def _():
            for off in range(1, n_chaos):
                greet({"mesh": other, "chaos": peer_c(off)})

    neighbours = jnp.where(has_low, 1, 0) + jnp.where(has_up, 1, 0)
    pl.semaphore_wait(
        barrier, n_chaos - 1 + n_mesh - 1 + n_kl - 1 + neighbours * (n_chaos - 1)
    )

    def remote(src, dst, send, recv, target):
        return pltpu.make_async_remote_copy(
            src_ref=src, dst_ref=dst, send_sem=send, recv_sem=recv,
            device_id=target, device_id_type=MESH,
        )

    elem_at = pl.multiple_of(c * elems, 128)
    mine = pl.ds(elem_at, elems)
    pending = []

    coef_waits = []
    for off in range(1, n_kl):
        copy = remote(
            coef_in.at[:, mine], coefs.at[k], sem_cs.at[off], sem_cr.at[off],
            {"kl": lax.rem(k + off, n_kl)},
        )
        copy.start()
        pending.append((None, copy))
        source = lax.rem(k + n_kl - off, n_kl)
        coef_waits.append(
            remote(coef_in.at[:, mine], coefs.at[source], sem_cs.at[off], sem_cr.at[off],
                   {"kl": lax.rem(k + off, n_kl)})
        )
    gather_waits = []
    for off in range(1, n_chaos):
        for which, ref in enumerate((rhs_in, pre_in)):
            target = {"chaos": peer_c(off)}
            sems = (sem_gs.at[off, which], sem_gr.at[off, which])
            copy = remote(ref, gathered.at[which, c], *sems, target)
            copy.start()
            pending.append((None, copy))
            gather_waits.append(remote(ref, gathered.at[which, source_c(off)], *sems, target))
    coefs[k] = coef_in[:, mine]
    gathered[0, c] = rhs_in[...]
    gathered[1, c] = pre_in[...]

    hrow = jnp.concatenate([halo_in[0:1, :], halo_in[1:2, :]], axis=1)
    sub = lax.broadcasted_iota(jnp.int32, (node, 2 * halo), 0)
    hits = jnp.where(sub == hrow, 1.0, 0.0).astype(F32)
    halo_oh[...] = hits.astype(BF16)
    in_halo = jnp.sum(hits, axis=1, keepdims=True)

    dstack[...] = jnp.zeros_like(dstack)
    dstack[0:mode_dev, :] = rhs_in[...]
    dstack[rd : rd + mode_dev, :] = pre_in[...]
    dstack[2 * rd : 2 * rd + 1, :] = mass_in[...]
    dsend[...] = fold(dot(split(dstack[...], 3), halo_oh[...]), dsend.shape[0])

    def to_sides(source_of, dst_of, send_of, recv_of):
        copies = []
        for side, has, other in sides:
            for off in range(n_chaos):
                copy = remote(
                    source_of(side), dst_of(1 - side, off),
                    send_of(side, off), recv_of(1 - side, off),
                    {"mesh": other, "chaos": peer_c(off)},
                )
                arrival = remote(
                    source_of(side), dst_of(side, off),
                    send_of(side, off), recv_of(side, off),
                    {"mesh": other, "chaos": peer_c(off)},
                )
                pl.when(has)(copy.start)
                pending.append((has, copy))
                copies.append((has, arrival))
        return copies

    zinit_waits = []
    for side, has, other in sides:
        for off in range(n_chaos):
            target = {"mesh": other, "chaos": peer_c(off)}
            copy = remote(dsend, zinit.at[1 - side, c], sem_zis.at[side, off],
                          sem_zir.at[1 - side, off], target)
            pl.when(has)(copy.start)
            pending.append((has, copy))
            zinit_waits.append(
                (has, remote(dsend, zinit.at[side, source_c(off)], sem_zis.at[side, off],
                             sem_zir.at[side, off], target))
            )

    square = 2 * halo
    spread = jnp.broadcast_to(hrow.astype(F32), (square, square))
    columns = jnp.transpose(spread).astype(jnp.int32)
    ids[0:node, :] = jnp.where(in_halo > 0.0, -1, sub)
    ghost = lax.broadcasted_iota(jnp.int32, (halo, square), 0) + node
    ids[low_at : low_at + halo, :] = ghost
    ids[low_at + halo : up_at, :] = columns[:halo]
    ids[up_at : up_at + halo, :] = ghost + halo
    ids[up_at + halo : wide, :] = columns[halo:]

    for corner in range(4):
        for tile in range(elems // 128):
            slots = conn_in[corner : corner + 1, pl.ds(elem_at + tile * 128, 128)]
            at = corner * elems + tile * 128
            oht[:, at : at + 128] = jnp.where(ids[...] == slots, 1.0, 0.0).astype(BF16)

    mix[...] = split(mix_in[...], 2)
    for buffer in range(2):
        if pairs > terms:
            sc_hi[buffer] = jnp.zeros_like(sc_hi[buffer])
            sc_lo[buffer] = jnp.zeros_like(sc_lo[buffer])

    for copy in coef_waits:
        copy.wait_recv()
    for copy in gather_waits:
        copy.wait_recv()
    for has, copy in zinit_waits:
        pl.when(has)(copy.wait_recv)

    lane = lax.broadcasted_iota(jnp.int32, (1, square), 1)
    first_half = lane < halo
    own_col = jnp.transpose(jnp.broadcast_to(in_halo, (node, 128)))[0:1]
    keep = jnp.where(own_col > 0.0, 0.0, 1.0)

    def blocks(dup, low, up):
        low = jnp.where(has_low, low, 0.0)
        up = jnp.where(has_up, up, 0.0)
        return (
            pltpu.roll(jnp.where(first_half, dup, low), halo, 1),
            jnp.where(first_half, up, dup),
        )

    base[...] = jnp.zeros_like(base)
    for which in range(2):
        for group in range(n_chaos):
            at = slice(group * mode_dev, (group + 1) * mode_dev)
            base[which, at, 0:node] = gathered[which, group]
            base[which, at, low_at:up_at] = zinit[0, group, which * rd : which * rd + mode_dev]
            base[which, at, up_at:wide] = zinit[1, group, which * rd : which * rd + mode_dev]
    for which in range(2):
        own = base[which, :, 0:node]
        dup = fold(dot(split(own, 3), halo_oh[...]), rows)
        low, up = blocks(dup, base[which, :, low_at:up_at], base[which, :, up_at:wide])
        base[which, :, 0:node] = own * keep
        base[which, :, low_at:up_at] = low
        base[which, :, up_at:wide] = up
    mass_dup = dsend[2 * rd : 2 * rd + 1, :]
    low, up = blocks(
        mass_dup, zinit[0, 0, 2 * rd : 2 * rd + 1, :], zinit[1, 0, 2 * rd : 2 * rd + 1, :]
    )
    mass_ext[:, 0:node] = mass_in[...]
    mass_ext[:, low_at:up_at] = low
    mass_ext[:, up_at:wide] = up

    lanes = lax.broadcasted_iota(jnp.int32, (1, wide), 1)
    counted = (lanes < node) | (lax.rem(lanes // halo, 2) == 1)
    counted = jnp.where(counted, 1.0, 0.0).astype(F32)

    def apply_local(vector, op):
        stacked = split(vector, 2)
        for step in range(elems // chunk):
            at = step * chunk
            here = pl.ds(elem_at + at, chunk)
            corners = [
                fold(dot(stacked, oht[:, b * elems + at : b * elems + at + chunk]), rows)
                for b in range(4)
            ]
            buffer = step % 2
            main = []
            for d in range(3):
                projected = grad_in[d, 0:1, here] * corners[0]
                for b in range(1, 4):
                    projected = projected + grad_in[d, b : b + 1, here] * corners[b]
                main.append(coefs[0, 0:1, at : at + chunk] * projected)
                for first in range(1, terms + 1, 2):
                    pair = []
                    for term in range(first, min(first + 2, terms + 1)):
                        group, entry = divmod(term, term_dev)
                        pair.append(coefs[group, entry : entry + 1, at : at + chunk] * projected)
                    while len(pair) < 2:
                        pair.append(jnp.zeros_like(projected))
                    both = jnp.concatenate(pair, axis=0)
                    high = both.astype(BF16)
                    to = slice((first - 1) * rows, (first + 1) * rows)
                    sc_hi[buffer, to, d * chunk : (d + 1) * chunk] = high
                    sc_lo[buffer, to, d * chunk : (d + 1) * chunk] = (
                        both - high.astype(F32)
                    ).astype(BF16)
            mixed = fold(dot(mix[...], sc_hi[buffer]), rows)
            mixed = mixed + dot(mix[...], sc_lo[buffer])[:rows]
            for a in range(4):
                local = None
                for d in range(3):
                    piece = grad_in[d, a : a + 1, here] * (
                        main[d] + mixed[:, d * chunk : (d + 1) * chunk]
                    )
                    local = piece if local is None else local + piece
                loc[:, a * elems + at : a * elems + at + chunk] = split(local, 2)
        part[op] = fold(dot_t(loc[...], oht[...]), rows)

    def send_parts(op):
        arrivals = []
        for off in range(1, n_chaos):
            copy = remote(part.at[op], from_x.at[op, off], sem_xs.at[op, off],
                          sem_xr.at[op, off], {"chaos": peer_c(off)})
            copy.start()
            pending.append((None, copy))
            arrivals.append((None, copy))
        spans = (slice(low_at, up_at), slice(up_at, wide))
        arrivals += to_sides(
            lambda side: part.at[op, :, spans[side]],
            lambda side, off: from_z.at[op, side, off],
            lambda side, off: sem_zs.at[op, side, off],
            lambda side, off: sem_zr.at[op, side, off],
        )
        return arrivals

    def finish(vector, op, arrivals):
        for has, copy in arrivals:
            if has is None:
                copy.wait_recv()
            else:
                pl.when(has)(copy.wait_recv)
        total = part[op]
        for off in range(1, n_chaos):
            total = total + from_x[op, off]
        edges = []
        for side, has, _ in sides:
            edge = from_z[op, side, 0]
            for off in range(1, n_chaos):
                edge = edge + from_z[op, side, off]
            edges.append(pltpu.roll(jnp.where(has, edge, 0.0), halo, 1))
        total = total + jnp.concatenate([jnp.zeros((rows, node), F32)] + edges, axis=1)
        return total + mass_ext[...] * vector

    def tile_sum(first, second):
        product = first * second * counted
        total = None
        for row in range(0, rows, 8):
            for at in range(0, wide, 128):
                piece = product[row : row + 8, at : at + 128]
                total = piece if total is None else total + piece
        return total

    def send_dots(step, residual, image, shared):
        dot_send[step, 0] = tile_sum(residual, shared)
        dot_send[step, 1] = tile_sum(image, shared)
        dot_recv[step, m] = dot_send[step]
        arrivals = []
        for off in range(1, n_mesh):
            target = {"mesh": lax.rem(m + off, n_mesh)}
            sems = (sem_ds.at[step, off], sem_dr.at[step, off])
            copy = remote(dot_send.at[step], dot_recv.at[step, m], *sems, target)
            copy.start()
            pending.append((None, copy))
            source = lax.rem(m + n_mesh - off, n_mesh)
            arrivals.append(remote(dot_send.at[step], dot_recv.at[step, source], *sems, target))
        return arrivals

    def take_dots(step, arrivals):
        for copy in arrivals:
            copy.wait_recv()
        total = dot_recv[step, 0]
        for source in range(1, n_mesh):
            total = total + dot_recv[step, source]
        sums = [
            jnp.sum(jnp.sum(total[i], axis=0, keepdims=True), axis=1, keepdims=True)
            for i in range(2)
        ]
        return sums

    residual = base[0]
    pre = base[1]
    shared = pre * residual
    apply_local(shared, 0)
    image = finish(shared, 0, send_parts(0))
    dir_image = dir_pre = dir_res = direction = None
    answer = None
    gamma_old = alpha_old = None
    for step in range(ITERS):
        dots = send_dots(step, residual, image, shared)
        last = step == ITERS - 1
        scaled = pre * image
        if not last:
            apply_local(scaled, step + 1)
            arrivals = send_parts(step + 1)
        gamma, delta = take_dots(step, dots)
        if step == 0:
            alpha = gamma / delta
            dir_pre, dir_res, direction = scaled, image, shared
            answer = alpha * direction
        else:
            beta = gamma / gamma_old
            alpha = gamma / (delta - beta * gamma / alpha_old)
            dir_pre = scaled + beta * dir_pre
            dir_res = image + beta * dir_res
            direction = shared + beta * direction
            answer = answer + alpha * direction
        residual = residual - alpha * dir_res
        shared = shared - alpha * dir_pre
        if not last:
            product = finish(scaled, step + 1, arrivals)
            dir_image = product if step == 0 else product + beta * dir_image
            image = image - alpha * dir_image
        gamma_old, alpha_old = gamma, alpha

    for out, value in ((x_out, answer), (res_out, residual)):
        dup = jnp.where(
            first_half, pltpu.roll(value[:, low_at:up_at], halo, 1), value[:, up_at:wide]
        )
        own = value[:, :node] + fold(dot_t(split(dup, 3), halo_oh[...]), rows)
        base[0, :, 0:node] = own
        for group in range(n_chaos):
            @pl.when(c == group)
            def _():
                out[...] = base[0, group * mode_dev : (group + 1) * mode_dev, 0:node]

    for has, copy in pending:
        if has is None:
            copy.wait_send()
        else:
            pl.when(has)(copy.wait_send)


def couple_terms(term_index, term_value, rows, pairs):
    mode_count = term_index.shape[-1]
    columns = lax.broadcasted_iota(jnp.int32, term_index.shape + (mode_count,), 3)
    table = jnp.sum(
        jnp.where(term_index[..., None] == columns, term_value[..., None], 0.0), axis=1
    )
    mirror = 0.5 * (table + jnp.swapaxes(table, 1, 2))
    pad = rows - mode_count
    mirror = jnp.pad(mirror, ((0, pairs - mirror.shape[0]), (0, pad), (0, pad)))
    return jnp.transpose(mirror, (1, 0, 2)).reshape(rows, pairs * rows)


def per_device(
    right_side,
    preconditioner,
    mass_diag,
    halo_lists,
    connectivity,
    gradients,
    coefficient,
    term_index,
    term_value,
):
    n_mesh, n_chaos, n_kl = (lax.axis_size(axis) for axis in ("mesh", "chaos", "kl"))
    mode_dev, node = right_side.shape
    modes = mode_dev * n_chaos
    halo = halo_lists.shape[1]
    elem_dev = connectivity.shape[1]
    term_dev = coefficient.shape[0]
    terms = term_dev * n_kl - 1
    rows, rd, pairs = round_up(modes, 8), round_up(mode_dev, 8), round_up(terms, 2)
    elems = round_up(-(-elem_dev // n_chaos), 128)
    chunk = 256 if elems % 256 == 0 else 128
    wide = node + 4 * halo
    extra = elems * n_chaos - elem_dev
    if extra:
        connectivity = jnp.pad(connectivity, ((0, 0), (0, extra)))
        gradients = jnp.pad(gradients, ((0, 0), (0, 0), (0, extra)))
        coefficient = jnp.pad(coefficient, ((0, 0), (0, extra)))
    mix = couple_terms(term_index, term_value, rows, pairs)
    dims = (n_mesh, n_chaos, n_kl, modes, mode_dev, node, halo, elems, chunk, terms, term_dev)
    vmem = pltpu.VMEM
    dma = pltpu.SemaphoreType.DMA
    drows = 2 * rd + 8
    return pl.pallas_call(
        functools.partial(kernel, dims),
        out_shape=[jax.ShapeDtypeStruct((mode_dev, node), F32)] * 2,
        in_specs=[pl.BlockSpec(memory_space=vmem)] * 8,
        out_specs=[pl.BlockSpec(memory_space=vmem)] * 2,
        scratch_shapes=[
            vmem((2, n_chaos, mode_dev, node), F32),
            vmem((n_kl, term_dev, elems), F32),
            vmem((drows, node), F32),
            vmem((drows, 2 * halo), F32),
            vmem((2, n_chaos, drows, 2 * halo), F32),
            vmem((wide, 2 * halo), jnp.int32),
            vmem((wide, 4 * elems), BF16),
            vmem((node, 2 * halo), BF16),
            vmem((2, rows, wide), F32),
            vmem((1, wide), F32),
            vmem((2 * rows, pairs * rows), BF16),
            vmem((2, pairs * rows, 3 * chunk), BF16),
            vmem((2, pairs * rows, 3 * chunk), BF16),
            vmem((2 * rows, 4 * elems), BF16),
            vmem((OPS, rows, wide), F32),
            vmem((OPS, n_chaos, rows, wide), F32),
            vmem((OPS, 2, n_chaos, rows, 2 * halo), F32),
            vmem((ITERS, 2, 8, 128), F32),
            vmem((ITERS, n_mesh, 2, 8, 128), F32),
            dma((n_chaos, 2)),
            dma((n_chaos, 2)),
            dma((n_kl,)),
            dma((n_kl,)),
            dma((2, n_chaos)),
            dma((2, n_chaos)),
            dma((OPS, n_chaos)),
            dma((OPS, n_chaos)),
            dma((OPS, 2, n_chaos)),
            dma((OPS, 2, n_chaos)),
            dma((ITERS, n_mesh)),
            dma((ITERS, n_mesh)),
        ],
        compiler_params=pltpu.CompilerParams(
            collective_id=0, has_side_effects=True, vmem_limit_bytes=56 * 2**20
        ),
    )(
        right_side,
        preconditioner,
        mass_diag.reshape(1, node),
        halo_lists,
        connectivity,
        gradients,
        coefficient,
        mix,
    )


def solution(mesh):
    return jax.shard_map(
        per_device,
        mesh=mesh,
        in_specs=(
            P(("grp", "chaos"), "mesh"),
            P("chaos", "mesh"),
            P("mesh"),
            P(None, "mesh"),
            P(None, "mesh"),
            P(None, None, "mesh"),
            P(("grp", "kl"), "mesh"),
            P(),
            P(),
        ),
        out_specs=(P(("grp", "chaos"), "mesh"), P(("grp", "chaos"), "mesh")),
        check_vma=False,
    )
```

```python
import functools

import jax
import jax.numpy as jnp
from jax import lax
from jax.experimental import pallas as pl
from jax.experimental.pallas import tpu as pltpu
from jax.sharding import PartitionSpec as P

ITERS = 3
OPS = ITERS
F32 = jnp.float32
BF16 = jnp.bfloat16
MESH = pl.DeviceIdType.MESH


def round_up(value, unit):
    return -(-value // unit) * unit


def split(value, parts):
    pieces = []
    rest = value
    for _ in range(parts - 1):
        high = rest.astype(BF16).astype(F32)
        pieces.append(high)
        rest = rest - high
    pieces.append(rest)
    return jnp.concatenate(pieces, axis=0).astype(BF16)


def fold(value, rows):
    total = value[:rows]
    for start in range(rows, value.shape[0], rows):
        total = total + value[start : start + rows]
    return total


def dot(left, right):
    return lax.dot_general(left, right, (((1,), (0,)), ((), ())), preferred_element_type=F32)


def dot_t(left, right):
    return lax.dot_general(left, right, (((1,), (1,)), ((), ())), preferred_element_type=F32)


def kernel(
    dims,
    rhs_in,
    pre_in,
    mass_in,
    halo_in,
    conn_in,
    grad_in,
    coef_in,
    index_in,
    value_in,
    out,
    gathered,
    coefs,
    mass_buf,
    halo_buf,
    conn,
    grad,
    index_buf,
    value_buf,
    dstack,
    dsend,
    zinit,
    ids,
    id_row,
    oht,
    oh,
    halo_oh,
    base,
    mass_ext,
    table,
    stack,
    mix,
    sc_hi,
    sc_lo,
    loc,
    mine_part,
    from_k,
    part,
    from_x,
    from_z,
    dot_send,
    dot_recv,
    last_send,
    last_recv,
    sem_in,
    sem_gs,
    sem_gr,
    sem_cs,
    sem_cr,
    sem_zis,
    sem_zir,
    sem_xs,
    sem_xr,
    sem_zs,
    sem_zr,
    sem_ds,
    sem_dr,
    sem_ks,
    sem_kr,
    sem_ls,
    sem_lr,
):
    n_mesh, n_chaos, n_kl, modes, mode_dev, node, halo, elems, terms, term_dev = dims
    rows = round_up(modes, 8)
    rd = round_up(mode_dev, 8)
    pairs = round_up(terms, 2)
    wide = node + 4 * halo
    low_at, up_at = node, node + 2 * halo

    m = lax.axis_index("mesh")
    c = lax.axis_index("chaos")
    k = lax.axis_index("kl")
    has_low = m > 0
    has_up = m < n_mesh - 1
    sides = ((0, has_low, m - 1), (1, has_up, m + 1))

    def peer_c(off):
        return lax.rem(c + off, n_chaos)

    def source_c(off):
        return lax.rem(c + n_chaos - off, n_chaos)

    barrier = pltpu.get_barrier_semaphore()

    def greet(target):
        pl.semaphore_signal(barrier, inc=1, device_id=target, device_id_type=MESH)

    plane = [(a, b) for a in range(n_mesh) for b in range(n_chaos) if a or b]
    for mesh_off, off in plane:
        greet({"mesh": lax.rem(m + mesh_off, n_mesh), "chaos": peer_c(off)})
    for off in range(1, n_kl):
        greet({"kl": lax.rem(k + off, n_kl)})

    def remote(src, dst, send, recv, target):
        return pltpu.make_async_remote_copy(
            src_ref=src, dst_ref=dst, send_sem=send, recv_sem=recv,
            device_id=target, device_id_type=MESH,
        )

    def share(kl_index):
        return pl.ds(pl.multiple_of((c * n_kl + kl_index) * elems, 128), elems)

    mine = share(k)
    pending = []
    loads = [
        pltpu.make_async_copy(src, dst, sem_in.at[at])
        for at, (src, dst) in enumerate(
            (
                (halo_in, halo_buf),
                (rhs_in, gathered.at[0, c]),
                (pre_in, gathered.at[1, c]),
                (mass_in, mass_buf),
                (conn_in.at[:, mine], conn),
                (index_in, index_buf),
                (value_in, value_buf),
                (grad_in.at[:, :, mine], grad),
                (coef_in.at[:, mine], coefs.at[k]),
            )
        )
    ]
    for load in loads:
        load.start()
    for load in loads[:4]:
        load.wait()

    hrow = jnp.concatenate([halo_buf[0:1, :], halo_buf[1:2, :]], axis=1)
    sub = lax.broadcasted_iota(jnp.int32, (node, 2 * halo), 0)
    hits = jnp.where(sub == hrow, 1.0, 0.0).astype(F32)
    halo_oh[...] = hits.astype(BF16)
    in_halo = jnp.sum(hits, axis=1, keepdims=True)

    dstack[...] = jnp.zeros_like(dstack)
    dstack[0:mode_dev, :] = gathered[0, c]
    dstack[rd : rd + mode_dev, :] = gathered[1, c]
    dstack[2 * rd : 2 * rd + 1, :] = mass_buf[...]
    dsend[...] = fold(dot(split(dstack[...], 3), halo_oh[...]), dsend.shape[0])

    pl.semaphore_wait(barrier, len(plane) + n_kl - 1)

    gather_waits = []
    for off in range(1, n_chaos):
        for which, ref in enumerate((rhs_in, pre_in)):
            target = {"chaos": peer_c(off)}
            sems = (sem_gs.at[off, which], sem_gr.at[off, which])
            copy = remote(ref, gathered.at[which, c], *sems, target)
            copy.start()
            pending.append((None, copy))
            gather_waits.append(remote(ref, gathered.at[which, source_c(off)], *sems, target))

    def to_sides(source_of, dst_of, send_of, recv_of):
        copies = []
        for side, has, other in sides:
            for off in range(n_chaos):
                copy = remote(
                    source_of(side), dst_of(1 - side, off),
                    send_of(side, off), recv_of(1 - side, off),
                    {"mesh": other, "chaos": peer_c(off)},
                )
                arrival = remote(
                    source_of(side), dst_of(side, off),
                    send_of(side, off), recv_of(side, off),
                    {"mesh": other, "chaos": peer_c(off)},
                )
                pl.when(has)(copy.start)
                pending.append((has, copy))
                copies.append((has, arrival))
        return copies

    zinit_waits = []
    for side, has, other in sides:
        for off in range(n_chaos):
            target = {"mesh": other, "chaos": peer_c(off)}
            copy = remote(dsend, zinit.at[1 - side, c], sem_zis.at[side, off],
                          sem_zir.at[1 - side, off], target)
            pl.when(has)(copy.start)
            pending.append((has, copy))
            zinit_waits.append(
                (has, remote(dsend, zinit.at[side, source_c(off)], sem_zis.at[side, off],
                             sem_zir.at[side, off], target))
            )

    coef_waits = []
    for off in range(1, n_kl):
        target = lax.rem(k + off, n_kl)
        sems = (sem_cs.at[off], sem_cr.at[off])
        copy = remote(coef_in.at[:, share(target)], coefs.at[k], *sems, {"kl": target})
        copy.start()
        pending.append((None, copy))
        source = lax.rem(k + n_kl - off, n_kl)
        coef_waits.append(
            remote(coef_in.at[:, mine], coefs.at[source], *sems, {"kl": target})
        )

    square = 2 * halo
    lane = lax.broadcasted_iota(jnp.int32, (1, square), 1)
    first_half = lane < halo
    own_col = jnp.transpose(jnp.broadcast_to(in_halo, (node, 128)))[0:1]
    spread = jnp.broadcast_to(hrow.astype(F32), (square, square))
    columns = jnp.transpose(spread).astype(jnp.int32)
    ids[0:node, :] = jnp.where(in_halo > 0.0, -1, sub)
    ghost = lax.broadcasted_iota(jnp.int32, (halo, square), 0) + node
    ids[low_at : low_at + halo, :] = ghost
    ids[low_at + halo : up_at, :] = columns[:halo]
    ids[up_at : up_at + halo, :] = ghost + halo
    ids[up_at + halo : wide, :] = columns[halo:]
    node_lane = lax.broadcasted_iota(jnp.int32, (1, node), 1)
    id_row[:, 0:node] = jnp.where(own_col > 0.0, -1, node_lane)
    id_row[:, low_at:up_at] = jnp.where(first_half, node + lane, pltpu.roll(hrow, halo, 1))
    id_row[:, up_at:wide] = jnp.where(first_half, node + halo + lane, hrow)

    tiles = elems // 128
    loads[4].wait()
    for tile in range(tiles):
        for corner in range(4):
            slots = conn[corner : corner + 1, tile * 128 : (tile + 1) * 128]
            at = (tile * 4 + corner) * 128
            oht[:, at : at + 128] = jnp.where(ids[...] == slots, 1.0, 0.0).astype(BF16)
            down = jnp.transpose(jnp.broadcast_to(slots, (128, 128)))
            for start in range(0, wide, 128):
                there = slice(start, start + 128)
                oh[at : at + 128, there] = jnp.where(
                    down == id_row[:, there], 1.0, 0.0
                ).astype(BF16)

    loads[5].wait()
    loads[6].wait()
    table[...] = jnp.zeros_like(table)
    stack[...] = jnp.zeros_like(stack)
    packed = table.shape[2]
    mode_sub = lax.broadcasted_iota(jnp.int32, (rows, stack.shape[1]), 0).astype(F32) + 1.0
    flat = None
    for term in range(terms):
        table[term, 0:2, 0:modes] = index_buf[term].astype(F32) + 1.0
        table[term, 2:4, 0:modes] = value_buf[term]
        entry = table[term]
        moved = pltpu.roll(entry, term * rows, 1) if term else entry
        flat = moved if flat is None else flat + moved
        block = None
        for slot in range(2):
            here = slice(0, stack.shape[1])
            piece = jnp.where(
                entry[slot : slot + 1, here] == mode_sub, entry[slot + 2 : slot + 3, here], 0.0
            )
            block = piece if block is None else block + piece
        stack[term * rows : (term + 1) * rows, :] = block
    both_ways = jnp.transpose(stack[...])[:rows]
    flat_sub = lax.broadcasted_iota(jnp.int32, (rows, packed), 0).astype(F32) + 1.0
    for slot in range(2):
        both_ways = both_ways + jnp.where(
            flat[slot : slot + 1] == flat_sub, flat[slot + 2 : slot + 3], 0.0
        )
    mix[...] = split(0.5 * both_ways, 2)
    sc_hi[...] = jnp.zeros_like(sc_hi)
    sc_lo[...] = jnp.zeros_like(sc_lo)

    loads[7].wait()
    loads[8].wait()
    for copy in coef_waits:
        copy.wait_recv()
    for copy in gather_waits:
        copy.wait_recv()
    for has, copy in zinit_waits:
        pl.when(has)(copy.wait_recv)

    keep = jnp.where(own_col > 0.0, 0.0, 1.0)

    def blocks(dup, low, up):
        low = jnp.where(has_low, low, 0.0)
        up = jnp.where(has_up, up, 0.0)
        return (
            pltpu.roll(jnp.where(first_half, dup, low), halo, 1),
            jnp.where(first_half, up, dup),
        )

    base[...] = jnp.zeros_like(base)
    for which in range(2):
        for group in range(n_chaos):
            at = slice(group * mode_dev, (group + 1) * mode_dev)
            base[which, at, 0:node] = gathered[which, group]
            base[which, at, low_at:up_at] = zinit[0, group, which * rd : which * rd + mode_dev]
            base[which, at, up_at:wide] = zinit[1, group, which * rd : which * rd + mode_dev]
    for which in range(2):
        own = base[which, :, 0:node]
        dup = fold(dot(split(own, 3), halo_oh[...]), rows)
        low, up = blocks(dup, base[which, :, low_at:up_at], base[which, :, up_at:wide])
        base[which, :, 0:node] = own * keep
        base[which, :, low_at:up_at] = low
        base[which, :, up_at:wide] = up
    mass_dup = dsend[2 * rd : 2 * rd + 1, :]
    low, up = blocks(
        mass_dup, zinit[0, 0, 2 * rd : 2 * rd + 1, :], zinit[1, 0, 2 * rd : 2 * rd + 1, :]
    )
    mass_ext[:, 0:node] = mass_buf[...]
    mass_ext[:, low_at:up_at] = low
    mass_ext[:, up_at:wide] = up

    lanes = lax.broadcasted_iota(jnp.int32, (1, wide), 1)
    counted = (lanes < node) | (lax.rem(lanes // halo, 2) == 1)
    counted = jnp.where(counted, 1.0, 0.0).astype(F32)

    def apply_local(vector, op):
        stacked = split(vector, 2)
        main = []
        for tile in range(tiles):
            here = slice(tile * 128, (tile + 1) * 128)
            picked = fold(dot(stacked, oht[:, tile * 512 : (tile + 1) * 512]), rows)
            for d in range(3):
                projected = None
                for b in range(4):
                    piece = grad[d, b : b + 1, here] * picked[:, b * 128 : (b + 1) * 128]
                    projected = piece if projected is None else projected + piece
                main.append(coefs[0, 0:1, here] * projected)
                to = slice((tile * 3 + d) * 128, (tile * 3 + d + 1) * 128)
                for first in range(1, terms + 1, 2):
                    pair = []
                    for term in range(first, min(first + 2, terms + 1)):
                        group, entry = divmod(term, term_dev)
                        pair.append(coefs[group, entry : entry + 1, here] * projected)
                    while len(pair) < 2:
                        pair.append(jnp.zeros_like(projected))
                    both = jnp.concatenate(pair, axis=0)
                    high = both.astype(BF16)
                    down = slice((first - 1) * rows, (first + 1) * rows)
                    sc_hi[down, to] = high
                    sc_lo[down, to] = (both - high.astype(F32)).astype(BF16)
        mixed = fold(dot(mix[...], sc_hi[...]), rows)
        mixed = mixed + dot(mix[...], sc_lo[...])[:rows]
        for tile in range(tiles):
            here = slice(tile * 128, (tile + 1) * 128)
            flows = [
                main[tile * 3 + d] + mixed[:, (tile * 3 + d) * 128 : (tile * 3 + d + 1) * 128]
                for d in range(3)
            ]
            for a in range(4):
                local = None
                for d in range(3):
                    piece = grad[d, a : a + 1, here] * flows[d]
                    local = piece if local is None else local + piece
                at = (tile * 4 + a) * 128
                loc[:, at : at + 128] = split(local, 2)
        mine_part[op] = fold(dot(loc[...], oh[...]), rows)
        copies = []
        for off in range(1, n_kl):
            copy = remote(mine_part.at[op], from_k.at[op, off], sem_ks.at[op, off],
                          sem_kr.at[op, off], {"kl": lax.rem(k + off, n_kl)})
            copy.start()
            pending.append((None, copy))
            copies.append(copy)
        total = mine_part[op]
        for off, copy in enumerate(copies, 1):
            copy.wait_recv()
            total = total + from_k[op, off]
        part[op] = total

    def send_parts(op):
        arrivals = []
        for off in range(1, n_chaos):
            copy = remote(part.at[op], from_x.at[op, off], sem_xs.at[op, off],
                          sem_xr.at[op, off], {"chaos": peer_c(off)})
            copy.start()
            pending.append((None, copy))
            arrivals.append((None, copy))
        spans = (slice(low_at, up_at), slice(up_at, wide))
        arrivals += to_sides(
            lambda side: part.at[op, :, spans[side]],
            lambda side, off: from_z.at[op, side, off],
            lambda side, off: sem_zs.at[op, side, off],
            lambda side, off: sem_zr.at[op, side, off],
        )
        return arrivals

    def finish(vector, op, arrivals):
        for has, copy in arrivals:
            if has is None:
                copy.wait_recv()
            else:
                pl.when(has)(copy.wait_recv)
        total = part[op]
        for off in range(1, n_chaos):
            total = total + from_x[op, off]
        edges = []
        for side, has, _ in sides:
            edge = from_z[op, side, 0]
            for off in range(1, n_chaos):
                edge = edge + from_z[op, side, off]
            edges.append(pltpu.roll(jnp.where(has, edge, 0.0), halo, 1))
        total = total + jnp.concatenate([jnp.zeros((rows, node), F32)] + edges, axis=1)
        return total + mass_ext[...] * vector

    def tile_sum(first, second):
        product = first * second
        total = None
        for row in range(0, rows, 8):
            for at in range(0, wide, 128):
                piece = product[row : row + 8, at : at + 128]
                total = piece if total is None else total + piece
        return total

    def send_dots(step, residual, image, shared):
        seen = shared * counted
        dot_send[step, 0] = tile_sum(residual, seen)
        dot_send[step, 1] = tile_sum(image, seen)
        dot_recv[step, m] = dot_send[step]
        arrivals = []
        for off in range(1, n_mesh):
            target = {"mesh": lax.rem(m + off, n_mesh)}
            sems = (sem_ds.at[step, off], sem_dr.at[step, off])
            copy = remote(dot_send.at[step], dot_recv.at[step, m], *sems, target)
            copy.start()
            pending.append((None, copy))
            source = lax.rem(m + n_mesh - off, n_mesh)
            arrivals.append(remote(dot_send.at[step], dot_recv.at[step, source], *sems, target))
        return arrivals

    def take_dots(step, arrivals):
        for copy in arrivals:
            copy.wait_recv()
        total = dot_recv[step, 0]
        for source in range(1, n_mesh):
            total = total + dot_recv[step, source]
        return sum_both(total)

    def sum_both(total):
        sums = [
            jnp.sum(jnp.sum(total[i], axis=0, keepdims=True), axis=1, keepdims=True)
            for i in range(2)
        ]
        return sums

    def send_last(gamma_tile, delta_tile):
        last_send[0] = gamma_tile
        last_send[1] = delta_tile
        last_recv[m * n_chaos + c] = last_send[...]
        arrivals = []
        for at, (mesh_off, off) in enumerate(plane):
            target = {"mesh": lax.rem(m + mesh_off, n_mesh), "chaos": peer_c(off)}
            sems = (sem_ls.at[at], sem_lr.at[at])
            copy = remote(last_send, last_recv.at[m * n_chaos + c], *sems, target)
            copy.start()
            pending.append((None, copy))
            source = lax.rem(m + n_mesh - mesh_off, n_mesh) * n_chaos + source_c(off)
            arrivals.append(remote(last_send, last_recv.at[source], *sems, target))
        return arrivals

    def take_last(arrivals):
        for copy in arrivals:
            copy.wait_recv()
        total = last_recv[0]
        for source in range(1, n_mesh * n_chaos):
            total = total + last_recv[source]
        return sum_both(total)

    residual = base[0]
    pre = base[1]
    shared = pre * residual
    apply_local(shared, 0)
    image = finish(shared, 0, send_parts(0))
    dir_image = dir_pre = dir_res = direction = None
    answer = None
    gamma_old = alpha_old = None
    for step in range(ITERS):
        last = step == ITERS - 1
        if step == 0 or not last:
            dots = send_dots(step, residual, image, shared)
        scaled = pre * image
        if not last:
            apply_local(scaled, step + 1)
            arrivals = send_parts(step + 1)
        gamma, delta = take_last(dots) if last and step else take_dots(step, dots)
        if step == 0:
            alpha = gamma / delta
            dir_pre, dir_res, direction = scaled, image, shared
            answer = alpha * direction
        else:
            beta = gamma / gamma_old
            alpha = gamma / (delta - beta * gamma / alpha_old)
            dir_pre = scaled + beta * dir_pre
            dir_res = image + beta * dir_res
            direction = shared + beta * direction
            answer = answer + alpha * direction
        residual = residual - alpha * dir_res
        shared = shared - alpha * dir_pre
        if step and step == ITERS - 2:
            seen = shared * counted
            rest = image - alpha * (beta * dir_image + mass_ext[...] * scaled)
            first_group = jnp.where(c == 0, 1.0, 0.0).astype(F32)
            dots = send_last(
                first_group * tile_sum(residual, seen),
                first_group * tile_sum(rest, seen)
                - alpha * tile_sum(part[step + 1], shared),
            )
        if not last:
            product = finish(scaled, step + 1, arrivals)
            dir_image = product if step == 0 else product + beta * dir_image
            image = image - alpha * dir_image
        gamma_old, alpha_old = gamma, alpha

    for at, value in enumerate((answer, residual)):
        dup = jnp.where(
            first_half, pltpu.roll(value[:, low_at:up_at], halo, 1), value[:, up_at:wide]
        )
        own = value[:, :node] + fold(dot_t(split(dup, 3), halo_oh[...]), rows)
        base[0, :, 0:node] = own
        for group in range(n_chaos):
            @pl.when(c == group)
            def _():
                out[at] = base[0, group * mode_dev : (group + 1) * mode_dev, 0:node]

    for has, copy in pending:
        if has is None:
            copy.wait_send()
        else:
            pl.when(has)(copy.wait_send)


def per_device(
    right_side,
    preconditioner,
    mass_diag,
    halo_lists,
    connectivity,
    gradients,
    coefficient,
    term_index,
    term_value,
):
    n_mesh, n_chaos, n_kl = (lax.axis_size(axis) for axis in ("mesh", "chaos", "kl"))
    mode_dev, node = right_side.shape
    modes = mode_dev * n_chaos
    halo = halo_lists.shape[1]
    elem_dev = connectivity.shape[1]
    term_dev = coefficient.shape[0]
    terms = term_dev * n_kl - 1
    rows, rd, pairs = round_up(modes, 8), round_up(mode_dev, 8), round_up(terms, 2)
    elems = round_up(-(-elem_dev // (n_chaos * n_kl)), 128)
    wide = node + 4 * halo
    extra = elems * n_chaos * n_kl - elem_dev
    if extra:
        connectivity = jnp.pad(connectivity, ((0, 0), (0, extra)))
        gradients = jnp.pad(gradients, ((0, 0), (0, 0), (0, extra)))
        coefficient = jnp.pad(coefficient, ((0, 0), (0, extra)))
    packed = round_up(pairs * rows, 128)
    dims = (n_mesh, n_chaos, n_kl, modes, mode_dev, node, halo, elems, terms, term_dev)
    vmem = pltpu.VMEM
    dma = pltpu.SemaphoreType.DMA
    drows = 2 * rd + 8
    both = pl.pallas_call(
        functools.partial(kernel, dims),
        out_shape=jax.ShapeDtypeStruct((2, mode_dev, node), F32),
        in_specs=[pl.BlockSpec(memory_space=pl.ANY)] * 9,
        out_specs=pl.BlockSpec(memory_space=vmem),
        scratch_shapes=[
            vmem((2, n_chaos, mode_dev, node), F32),
            vmem((n_kl, term_dev, elems), F32),
            vmem((1, node), F32),
            vmem((2, halo), jnp.int32),
            vmem((4, elems), jnp.int32),
            vmem((3, 4, elems), F32),
            vmem(term_index.shape, jnp.int32),
            vmem(term_value.shape, F32),
            vmem((drows, node), F32),
            vmem((drows, 2 * halo), F32),
            vmem((2, n_chaos, drows, 2 * halo), F32),
            vmem((wide, 2 * halo), jnp.int32),
            vmem((1, wide), jnp.int32),
            vmem((wide, 4 * elems), BF16),
            vmem((4 * elems, wide), BF16),
            vmem((node, 2 * halo), BF16),
            vmem((2, rows, wide), F32),
            vmem((1, wide), F32),
            vmem((terms, 8, packed), F32),
            vmem((packed, round_up(rows, 128)), F32),
            vmem((2 * rows, packed), BF16),
            vmem((packed, 3 * elems), BF16),
            vmem((packed, 3 * elems), BF16),
            vmem((2 * rows, 4 * elems), BF16),
            vmem((OPS, rows, wide), F32),
            vmem((OPS, n_kl, rows, wide), F32),
            vmem((OPS, rows, wide), F32),
            vmem((OPS, n_chaos, rows, wide), F32),
            vmem((OPS, 2, n_chaos, rows, 2 * halo), F32),
            vmem((ITERS, 2, 8, 128), F32),
            vmem((ITERS, n_mesh, 2, 8, 128), F32),
            vmem((2, 8, 128), F32),
            vmem((n_mesh * n_chaos, 2, 8, 128), F32),
            dma((9,)),
            dma((n_chaos, 2)),
            dma((n_chaos, 2)),
            dma((n_kl,)),
            dma((n_kl,)),
            dma((2, n_chaos)),
            dma((2, n_chaos)),
            dma((OPS, n_chaos)),
            dma((OPS, n_chaos)),
            dma((OPS, 2, n_chaos)),
            dma((OPS, 2, n_chaos)),
            dma((ITERS, n_mesh)),
            dma((ITERS, n_mesh)),
            dma((OPS, n_kl)),
            dma((OPS, n_kl)),
            dma((n_mesh * n_chaos,)),
            dma((n_mesh * n_chaos,)),
        ],
        compiler_params=pltpu.CompilerParams(
            collective_id=0, has_side_effects=True, vmem_limit_bytes=56 * 2**20
        ),
    )(
        right_side,
        preconditioner,
        mass_diag.reshape(1, node),
        halo_lists,
        connectivity,
        gradients,
        coefficient,
        term_index,
        term_value,
    )
    return both[0], both[1]


def solution(mesh):
    return jax.shard_map(
        per_device,
        mesh=mesh,
        in_specs=(
            P(("grp", "chaos"), "mesh"),
            P("chaos", "mesh"),
            P("mesh"),
            P(None, "mesh"),
            P(None, "mesh"),
            P(None, None, "mesh"),
            P(("grp", "kl"), "mesh"),
            P(),
            P(),
        ),
        out_specs=(P(("grp", "chaos"), "mesh"), P(("grp", "chaos"), "mesh")),
        check_vma=False,
    )
```
